768 devices in a mesh: sub: 32 (over y, x), col: 24 (over z, core).
Axes of the slice: x: 4, y: 8, z: 12, core: 2. Of those that a mesh axis runs over, the one named last changes fastest.
Arguments:
- inv_conductance: bfloat16 [2, 2048, 2048], P(None, 'sub'), may hold values from -1 to 1
- source: bfloat16 [96, 2, 2048], P('col', None, 'sub'), may hold values from -6 to 6
- line_ends: int32 [64, 2], replicated, may hold values from 0 to 4095, as said below
- delays: int32 [64], replicated, may hold values from 2 to 6
- admittance: float32 [64], replicated, may hold values from 0.3 to 1.2
- breaker: int32 [64, 96], P(None, 'col'), may hold values 0 or 1
- hist_volt: float32 [6, 96, 128], P(None, 'col'), may hold values from -4 to 4
- hist_inj: float32 [6, 96, 128], P(None, 'col'), may hold values from -4 to 4
- station_node: int32 [48], replicated, may hold values from 0 to 4095
- station_initial: float32 [96, 48], P(None, 'col'), may hold values from -4 to 4
- capacitor_initial: float32 [96, 48, 2400], P(None, 'col', 'sub'), may hold values from 0.6 to 1.4
- insert_count: int32 [8, 96, 48], P(None, None, 'col'), may hold values from 600 to 1800
Outputs:
- node_voltages: float32 [96, 2, 2048], P('col', None, 'sub')
- capacitor_volts: float32 [96, 48, 2400], P(None, 'col', 'sub')
- station_current: float32 [8, 96, 48], P(None, None, 'col')
The draws below stay inside these ranges and needn't reach their ends.
Inputs may be any that keep to these rules, and one draw needn't show every extreme that they name: `line_ends`: each line joins a node of one subnetwork to a node of another.
All inputs are finite; a program needn't handle non-finite values. No bound on the sum of `breaker` on one device may be relied on, other than what follows from the above.
Results may differ from the reference program's by a relative error of at most 0.0014.
Values may be sent and summed in bfloat16 or wider, within the bound.
A program may use at most 32 MiB of HBM per device.

```python
import math
import jax
import jax.numpy as jnp
from jax import lax

NS = 2048
C = 96
ST = 48
SM = 2400
SUBS = 2
STEPS = 8
DMIN = 2
DMAX = 6
LINES = 64
ENDS = 128


def draw_inv_conductance(key, part):
    key_off, key_diag = jax.random.split(key)
    off_diag = jnp.clip(jax.random.normal(key_off, (SUBS, NS, NS), jnp.float32), -4.0, 4.0)
    diagonal = jax.random.uniform(key_diag, (SUBS, NS, 1), jnp.float32, 0.3, 0.6)
    identity = (jnp.arange(NS)[:, None] == jnp.arange(NS)[None, :]).astype(jnp.float32)
    return (off_diag * (0.3 / math.sqrt(NS)) + identity * diagonal).astype(jnp.bfloat16)


def draw_line_ends(key, part):
    key_first, key_second, key_nodes = jax.random.split(key, 3)
    first_sub = jax.random.randint(key_first, (LINES,), 0, SUBS)
    second = jnp.mod(first_sub + jax.random.randint(key_second, (LINES,), 1, SUBS), SUBS)
    node_pick = jax.random.randint(key_nodes, (LINES, 2), 0, NS)
    joined = jnp.stack([first_sub * NS + node_pick[:, 0], second * NS + node_pick[:, 1]], axis=1)
    joined = joined.at[0, 0].set(0).at[0, 1].set(SUBS * NS - 1)
    return joined.astype(jnp.int32)


def draw_delays(key, part):
    picked = jax.random.randint(key, (LINES,), DMIN, DMAX + 1)
    picked = picked.at[0].set(DMIN).at[1].set(DMAX)
    return picked.astype(jnp.int32)


def set_ends(values, rng, smallest, largest):
    longest = values.shape.index(max(values.shape))
    spots = []
    for shift in (0, 1):
        where = [jax.random.randint(jax.random.fold_in(rng, axis), (), 0, length) for axis, length in enumerate(values.shape)]
        where[longest] = (where[longest] + shift) % values.shape[longest]
        spots.append(tuple(where))
    return values.at[spots[0]].set(smallest).at[spots[1]].set(largest)


def block_levels(rng, dims, pieces, smallest, top_value):
    gain = 1.0
    for dim, parts in pieces:
        draws = jax.random.uniform(jax.random.fold_in(jax.random.fold_in(rng, 6), dim), (parts,), jnp.float32, smallest / len(pieces), top_value / len(pieces))
        gain = gain * jnp.repeat(jnp.exp(draws), dims[dim] // parts).reshape((-1,) + (1,) * (len(dims) - 1 - dim))
    return gain


def centred(stream_key, extent, deviation, limit, cuts=(), held_as=jnp.bfloat16):
    array = deviation * jax.random.normal(stream_key, extent, jnp.float32)
    if cuts:
        array = array * block_levels(stream_key, extent, cuts, -0.22, 0.18)
    return jnp.clip(array, -limit, limit).astype(held_as)


def setup_inputs(seed: int = 0) -> dict:
    keys = jax.random.split(jax.random.key(seed), 13)
    return {
        "inv_conductance": draw_inv_conductance(jax.random.fold_in(keys[12], 71), 0),
        "source": centred(keys[1], (C, SUBS, NS), 1.0, 6.0, ((0, 24), (2, 32))),
        "line_ends": draw_line_ends(jax.random.fold_in(keys[12], 71), 0),
        "delays": draw_delays(jax.random.fold_in(keys[12], 71), 0),
        "admittance": jnp.clip(jnp.exp(jax.random.uniform(keys[4], (LINES,), jnp.float32, math.log(0.3), math.log(1.2))), 0.3, 1.2),
        "breaker": set_ends((jax.random.randint(keys[5], (LINES, C), 0, 4) < 3).astype(jnp.int32), jax.random.fold_in(keys[5], 1), 0, 1),
        "hist_volt": centred(keys[6], (DMAX, C, ENDS), 0.5, 4.0, ((1, 24),), jnp.float32),
        "hist_inj": centred(keys[7], (DMAX, C, ENDS), 0.5, 4.0, ((1, 24),), jnp.float32),
        "station_node": set_ends(jax.random.randint(keys[8], (ST,), 0, SUBS * NS), jax.random.fold_in(keys[8], 1), 0, (SUBS * NS) - 1).astype(jnp.int32),
        "station_initial": centred(keys[9], (C, ST), 0.5, 4.0, ((1, 24),), jnp.float32),
        "capacitor_initial": jnp.clip(0.6 + 0.79999995 * jax.random.uniform(keys[10], (C, ST, SM), jnp.float32) ** block_levels(keys[10], (C, ST, SM), ((1, 24), (2, 32)), -0.2, 0.2), 0.6, 1.4),
        "insert_count": set_ends(jax.random.randint(keys[11], (STEPS, C, ST), SM // 4, 3 * SM // 4 + 1), jax.random.fold_in(keys[11], 1), SM // 4, (3 * SM // 4 + 1) - 1).astype(jnp.int32),
    }


charge_rate = 0.5


def swap_ends(values):
    full_shape = values.shape
    paired = values.reshape(full_shape[:-1] + (full_shape[-1] // 2, 2))
    return paired[..., ::-1].reshape(full_shape)


def reference(inv_conductance, source, line_ends, delays, admittance, breaker, hist_volt, hist_inj, station_node, station_initial, capacitor_initial, insert_count):
    end_nodes = line_ends.reshape(-1)
    end_total = end_nodes.shape[0]
    end_delay = jnp.repeat(delays, 2)
    end_admit = jnp.repeat(admittance, 2)
    end_mask = jnp.repeat(breaker, 2, axis=0).T.astype(jnp.float32)
    volt_buffer = jnp.zeros((DMAX + STEPS, C, end_total), jnp.float32).at[:DMAX].set(hist_volt)
    inj_buffer = jnp.zeros((DMAX + STEPS, C, end_total), jnp.float32).at[:DMAX].set(hist_inj)
    matrix = inv_conductance.astype(jnp.float32)
    source_part = jnp.einsum("srk,csk->csr", matrix, source.astype(jnp.float32))
    position = jnp.arange(SM, dtype=jnp.int32)
    capacitor = capacitor_initial
    node_volt = station_initial
    currents = []
    voltages = source_part
    for step_index in range(STEPS):
        read_index = (step_index + DMAX - end_delay).astype(jnp.int32)
        selector = jnp.broadcast_to(read_index[None, None, :], (1, C, end_total))
        volt_read = jnp.take_along_axis(volt_buffer, selector, axis=0)[0]
        inj_read = jnp.take_along_axis(inj_buffer, selector, axis=0)[0]
        injection = end_mask * (2.0 * end_admit * swap_ends(volt_read) - swap_ends(inj_read))
        inj_buffer = inj_buffer.at[DMAX + step_index].set(injection)
        inserted_count = insert_count[step_index]
        inserted = (position < inserted_count[..., None]).astype(jnp.float32)
        thevenin = (2.0 / SM) * jnp.sum(inserted * capacitor, axis=-1)
        current = (thevenin - node_volt) / (1.0 + inserted_count.astype(jnp.float32) / SM)
        capacitor = capacitor - charge_rate * inserted * current[..., None]
        currents.append(current)
        term_full = jnp.zeros((C, SUBS * NS), jnp.float32)
        term_full = term_full.at[:, end_nodes].add(injection).at[:, station_node].add(current)
        term_full = lax.optimization_barrier(term_full.astype(jnp.bfloat16)).astype(jnp.float32)
        term_full = term_full.reshape(C, SUBS, NS)
        voltages = source_part + jnp.einsum("srk,csk->csr", matrix, term_full)
        flat_volts = voltages.reshape(C, SUBS * NS)
        volt_buffer = volt_buffer.at[DMAX + step_index].set(flat_volts[:, end_nodes])
        node_volt = flat_volts[:, station_node]
    return voltages, capacitor, jnp.stack(currents)
```

```python
import jax
import jax.numpy as jnp
from jax import lax
from jax.experimental import pallas as pl
from jax.experimental.pallas import tpu as pltpu
from jax.sharding import PartitionSpec as P

SM = 2400
STEPS = 8
DMIN = 2
DMAX = 6
NS = 2048
NX, NY, NC = 4, 8, 24
F32, BF16 = jnp.float32, jnp.bfloat16
MESH = pl.DeviceIdType.MESH
NT = (((1,), (1,)), ((), ()))


def split3(x):
    hi = x.astype(BF16).astype(F32)
    rest = x - hi
    mid = rest.astype(BF16).astype(F32)
    return hi, mid, rest - mid


def dot(a, b):
    return jnp.dot(a, b, preferred_element_type=F32)


def exact_dot(x, onehot):
    parts = jnp.concatenate([*split3(x), jnp.zeros_like(x)], axis=0)
    r = dot(parts.astype(BF16), onehot)
    return r[0:4] + r[4:8] + r[8:12]


def kernel(
    inv_ref, src_ref, ncol_ref, nrow_ref, msg0_ref, hv_ref, hj_ref, mask_ref, line_ref,
    volt_ref, cur_ref,
    gt_ref, s_ref, t_ref, send1y, buf1y, send1x, buf1x, wsend, wbuf, buf0, send2y, buf2y, send2x, buf2x, send3,
    s0, r0, s1y, r1y, s1x, r1x, sw, rw, s2y, r2y, s2x, r2x, s3, r3,
):
    sub, col = lax.axis_index("sub"), lax.axis_index("col")
    y, x = sub // NX, lax.rem(sub, NX)
    to_y = lambda p: {"sub": p * NX + x}
    to_x = lambda p: {"sub": y * NX + p}
    to_c = lambda p: {"col": p}

    def push(n, me, to, src, dst, send, recv):
        def body(d, carry):
            p = lax.rem(me + d, n)
            pltpu.make_async_remote_copy(
                src_ref=src(p), dst_ref=dst.at[me], send_sem=send.at[p], recv_sem=recv.at[me],
                device_id=to(p), device_id_type=MESH,
            ).start()
            return carry

        lax.fori_loop(1, n, body, 0)

    def copy_of(to, src, dst, send, recv, p):
        return pltpu.make_async_remote_copy(
            src_ref=src(p), dst_ref=dst.at[p], send_sem=send.at[p], recv_sem=recv.at[p],
            device_id=to(p), device_id_type=MESH,
        )

    def await_recv(n, me, to, src, dst, send, recv):
        def body(d, carry):
            copy_of(to, src, dst, send, recv, lax.rem(me + d, n)).wait_recv()
            return carry

        lax.fori_loop(1, n, body, 0)

    def await_send(n, me, to, src, dst, send, recv):
        def body(d, carry):
            copy_of(to, src, dst, send, recv, lax.rem(me + d, n)).wait_send()
            return carry

        lax.fori_loop(1, n, body, 0)

    barrier = pltpu.get_barrier_semaphore()
    for n, me, to in ((NC, col, to_c), (NY, y, to_y), (NX, x, to_x)):

        def greet(d, carry, n=n, me=me, to=to):
            pl.semaphore_signal(
                barrier, inc=1, device_id=to(lax.rem(me + d, n)), device_id_type=MESH
            )
            return carry

        lax.fori_loop(1, n, greet, 0)

    lane = lax.broadcasted_iota(jnp.int32, (1, 128), 1)
    low = lane < 64
    ncol = ncol_ref[...]
    ends_row, st_row = nrow_ref[:, 0:128], nrow_ref[:, 128:256]

    place = lax.rem(ncol[0:192], NS)
    acc = jnp.zeros((192, 128), F32)
    for k in range(0, NS, 512):
        spot = lax.broadcasted_iota(jnp.int32, (192, 512), 1) + k
        onehot = jnp.where(place == spot, 1.0, 0.0).astype(BF16)
        acc += lax.dot_general(onehot, inv_ref[:, k : k + 512], NT, preferred_element_type=F32)
    same_sub = jnp.where(ncol[0:192] >= NS, 1, 0) == jnp.where(low, 0, 1)
    gt = jnp.where(same_sub, acc, 0.0)
    gt_ref[...] = gt

    r = lax.broadcasted_iota(jnp.int32, (128, 1), 0)
    gid = jnp.where(r >= 64, NS - 64, 0) + r + sub * 64
    st_high = pltpu.roll(st_row, 64, 1)
    row0 = jnp.where(low, ends_row, st_high)
    row1 = jnp.where(low, pltpu.roll(ends_row, 64, 1), st_high)
    pick = jnp.where(gid == jnp.where(r >= 64, row1, row0), 1.0, 0.0).astype(BF16)
    mine = gt_ref[pl.ds(pl.multiple_of(col * 8, 8), 8), :]
    send1y[0:8, :] = dot(mine.astype(BF16), pick)
    send1y[8:12, :] = src_ref[...]
    send1y[12:16, :] = jnp.zeros((4, 128), F32)
    pl.semaphore_wait(barrier, NC + NY + NX - 3)

    ex1y = (NY, y, to_y, lambda p: send1y, buf1y, s1y, r1y)
    ex0 = (NC, col, to_c, lambda p: msg0_ref.at[p], buf0, s0, r0)
    push(*ex1y)
    push(*ex0)
    buf1y[y] = send1y[...]
    buf0[col] = msg0_ref[col]

    b_row = lax.broadcasted_iota(jnp.int32, (256, 256), 0)
    b_col = lax.broadcasted_iota(jnp.int32, (256, 256), 1)
    equal = ncol == nrow_ref[...]
    earlier = jnp.where(equal & (b_row < b_col), 1.0, 0.0)
    first = jnp.sum(earlier, axis=0, keepdims=True) == 0.0
    merge = jnp.where(equal & first, 1.0, 0.0).astype(BF16)
    at_ends = jnp.where(gid == ends_row, 1.0, 0.0).astype(BF16)
    at_st = jnp.where(gid == st_row, 1.0, 0.0).astype(BF16)

    await_recv(*ex1y)
    total = buf1y[0, 0:8]
    for p in range(1, NY):
        total += buf1y[p, 0:8]
    send1x[0:8, :] = total
    for p in range(NY):
        send1x[8 + 4 * p : 12 + 4 * p, :] = buf1y[p, 8:12]
    ex1x = (NX, x, to_x, lambda p: send1x, buf1x, s1x, r1x)
    push(*ex1x)
    buf1x[x] = send1x[...]

    await_recv(*ex0)
    t_ref[...] = jnp.zeros((128, 128), F32)
    for p in range(NC):
        t_ref[2 * p : 2 * p + 2, :] = buf0[p]
    stations = t_ref[...].T
    packed = jnp.where(low, stations[0:16], pltpu.roll(stations[16:32], 64, 1))

    await_recv(*ex1x)
    block = buf1x[0, 0:8]
    for p in range(1, NX):
        block += buf1x[p, 0:8]
    wsend[...] = block
    exw = (NC, col, to_c, lambda p: wsend, wbuf, sw, rw)
    push(*exw)
    wbuf[col] = block
    for p in range(NY):
        for q in range(NX // 2):
            a = buf1x[2 * q, 8 + 4 * p : 12 + 4 * p]
            b = buf1x[2 * q + 1, 8 + 4 * p : 12 + 4 * p]
            m = (2 * p + q) * 128
            s_ref[0:4, m : m + 128] = jnp.where(low, a, pltpu.roll(b, 64, 1))
            s_ref[4:8, m : m + 128] = jnp.where(low, pltpu.roll(a, 64, 1), b)
    both = lax.dot_general(s_ref[...].astype(BF16), inv_ref[...], NT, preferred_element_type=F32)
    source_part = jnp.where(low, both[0:4], both[4:8])
    send2y[0:16, :] = packed
    send2y[16:20, :] = exact_dot(source_part, at_ends)
    send2y[20:24, :] = exact_dot(source_part, at_st)
    ex2y = (NY, y, to_y, lambda p: send2y, buf2y, s2y, r2y)
    push(*ex2y)
    buf2y[y] = send2y[...]

    await_recv(*ex2y)
    total = buf2y[0]
    for p in range(1, NY):
        total += buf2y[p]
    send2x[...] = total
    ex2x = (NX, x, to_x, lambda p: send2x, buf2x, s2x, r2x)
    push(*ex2x)
    buf2x[x] = total

    await_recv(*exw)
    w = jnp.concatenate([wbuf[p] for p in range(NC)], axis=0)
    high_w = pltpu.roll(w, 64, 1)
    is_high = ncol[0:192] >= NS
    w_ends = jnp.where(low, jnp.where(is_high, 0.0, w), jnp.where(is_high, high_w, 0.0))
    w_st = jnp.where(low, high_w, 0.0)
    w_full = jnp.concatenate(
        [jnp.concatenate([w_ends, w_st], axis=1), jnp.zeros((64, 256), F32)], axis=0
    ).astype(BF16)

    await_recv(*ex2x)
    total = buf2x[0]
    for p in range(1, NX):
        total += buf2x[p]
    station_lane = lane < 48
    sums = jnp.where(
        station_lane,
        jnp.concatenate([total[0:16], pltpu.roll(total[0:16], 64, 1)], axis=0),
        0.0,
    )
    src_nodes = jnp.concatenate([total[16:20], total[20:24]], axis=1)

    volts = [hv_ref[t] for t in range(DMAX)]
    injs = [hj_ref[t] for t in range(DMAX)]
    counts = [jnp.where(station_lane, stations[32 + 4 * n : 36 + 4 * n], 0.0) for n in range(STEPS)]
    node_volt = jnp.where(station_lane, stations[64:68], 0.0)
    delay = line_ref[0:1, :]
    twice = 2.0 * line_ref[1:2, :]
    in_service = mask_ref[...]
    currents = []
    for n in range(STEPS):
        u, j = volts[n + DMAX - DMIN], injs[n + DMAX - DMIN]
        for d in range(DMIN + 1, DMAX + 1):
            at = delay == float(d)
            u = jnp.where(at, volts[n + DMAX - d], u)
            j = jnp.where(at, injs[n + DMAX - d], j)
        injection = in_service * (twice * pltpu.roll(u, 64, 1) - pltpu.roll(j, 64, 1))
        injs.append(injection)
        charge = sums[4 * n : 4 * n + 4]
        for q in range(n):
            charge -= 0.5 * jnp.minimum(counts[n], counts[q]) * currents[q]
        current = (2.0 / SM * charge - node_volt) / (1.0 + counts[n] / SM)
        current = jnp.where(station_lane, current, 0.0)
        currents.append(current)
        term = exact_dot(jnp.concatenate([injection, current], axis=1), merge)
        term = jnp.concatenate([term, jnp.zeros_like(term)], axis=0).astype(BF16)
        if n + 1 < STEPS:
            nodes = dot(term, w_full)[0:4] + src_nodes
            volts.append(nodes[:, 0:128])
            node_volt = nodes[:, 128:256]

    t_ref[0:32, :] = jnp.concatenate(currents, axis=0)
    t_ref[32:128, :] = jnp.zeros((96, 128), F32)
    out = t_ref[...].T
    for p in range(NC):
        send3[p] = out[2 * p : 2 * p + 2, :]
    ex3 = (NC, col, to_c, lambda p: send3.at[p], cur_ref, s3, r3)
    push(*ex3)
    cur_ref[col] = send3[col]
    last = dot(term, jnp.concatenate([gt, jnp.zeros((64, 128), F32)], axis=0).astype(BF16))
    volt_ref[...] = source_part + last[0:4]
    for ex in (ex0, ex1y, ex1x, exw, ex2y, ex2x):
        await_send(*ex)
    await_recv(*ex3)
    await_send(*ex3)


def exchange(inv, src, ncol, nrow, msg0, hv, hj, mask, line):
    vmem = pl.BlockSpec(memory_space=pltpu.VMEM)
    pairs = lambda n: [pltpu.SemaphoreType.DMA((n,)), pltpu.SemaphoreType.DMA((n,))]
    return pl.pallas_call(
        kernel,
        out_shape=(jax.ShapeDtypeStruct((4, 128), F32), jax.ShapeDtypeStruct((NC, 2, 128), F32)),
        in_specs=[vmem] * 9,
        out_specs=(vmem, vmem),
        scratch_shapes=[
            pltpu.VMEM((192, 128), F32),
            pltpu.VMEM((8, NS), F32),
            pltpu.VMEM((128, 128), F32),
            pltpu.VMEM((16, 128), F32),
            pltpu.VMEM((NY, 16, 128), F32),
            pltpu.VMEM((40, 128), F32),
            pltpu.VMEM((NX, 40, 128), F32),
            pltpu.VMEM((8, 128), F32),
            pltpu.VMEM((NC, 8, 128), F32),
            pltpu.VMEM((NC, 2, 128), F32),
            pltpu.VMEM((24, 128), F32),
            pltpu.VMEM((NY, 24, 128), F32),
            pltpu.VMEM((24, 128), F32),
            pltpu.VMEM((NX, 24, 128), F32),
            pltpu.VMEM((NC, 2, 128), F32),
            *pairs(NC), *pairs(NY), *pairs(NX), *pairs(NC), *pairs(NY), *pairs(NX), *pairs(NC),
        ],
        compiler_params=pltpu.CompilerParams(
            collective_id=0, has_side_effects=True, vmem_limit_bytes=24 * 1024 * 1024
        ),
    )(inv, src, ncol, nrow, msg0, hv, hj, mask, line)


def per_device(
    inv_conductance, source, line_ends, delays, admittance, breaker, hist_volt, hist_inj,
    station_node, station_initial, capacitor_initial, insert_count,
):
    sub_index = lax.axis_index("sub")
    flip = line_ends[:, 0] >= NS
    low_end = jnp.where(flip, line_ends[:, 1], line_ends[:, 0])
    high_end = jnp.where(flip, line_ends[:, 0], line_ends[:, 1])
    node = jnp.concatenate([low_end, high_end, station_node, -1 - jnp.arange(80, dtype=jnp.int32)])

    def by_sub(hist):
        paired = hist.reshape(DMAX, 4, 64, 2)
        even, odd = paired[..., 0], paired[..., 1]
        return jnp.concatenate([jnp.where(flip, odd, even), jnp.where(flip, even, odd)], axis=-1)

    mask = breaker.T.astype(F32)
    mask = jnp.concatenate([mask, mask], axis=1)
    line = jnp.stack([delays.astype(F32), admittance])
    line = jnp.concatenate([line, line], axis=1)

    position = sub_index * 75 + jnp.arange(75, dtype=jnp.int32)
    inserted = position < insert_count[..., None]
    part = jnp.sum(jnp.where(inserted, capacitor_initial, 0.0), axis=-1)
    to_owner = lambda v: v.reshape(STEPS, NC, 4, 2).transpose(1, 3, 0, 2).reshape(NC, 2, 32)
    first = station_initial.reshape(NC, 4, 2).transpose(0, 2, 1)
    msg0 = jnp.concatenate(
        [to_owner(part), to_owner(insert_count.astype(F32)), first, jnp.zeros((NC, 2, 60), F32)], axis=-1
    )
    volts, currents = exchange(
        inv_conductance.reshape(128, NS), source.astype(F32).reshape(4, 128), node[:, None], node[None, :],
        msg0, by_sub(hist_volt), by_sub(hist_inj), mask, line,
    )
    current = currents[:, :, :32].reshape(NC, 2, STEPS, 4).transpose(2, 0, 3, 1).reshape(STEPS, 96, 2)
    capacitor = capacitor_initial - 0.5 * jnp.sum(jnp.where(inserted, current[..., None], 0.0), axis=0)
    return volts.reshape(4, 2, 64), capacitor, current


def solution(mesh):
    in_specs = (
        P(None, "sub", None),
        P("col", None, "sub"),
        P(),
        P(),
        P(),
        P(None, "col"),
        P(None, "col", None),
        P(None, "col", None),
        P(),
        P(None, "col"),
        P(None, "col", "sub"),
        P(None, None, "col"),
    )
    out_specs = (P("col", None, "sub"), P(None, "col", "sub"), P(None, None, "col"))
    return jax.shard_map(
        per_device, mesh=mesh, in_specs=in_specs, out_specs=out_specs, check_vma=False
    )
```

```python
import jax
import jax.numpy as jnp
from jax import lax
from jax.experimental import pallas as pl
from jax.experimental.pallas import tpu as pltpu
from jax.sharding import PartitionSpec as P

SM = 2400
STEPS = 8
DMIN = 2
DMAX = 6
NS = 2048
NX, NY, NC = 4, 8, 24
F32, BF16 = jnp.float32, jnp.bfloat16
MESH = pl.DeviceIdType.MESH
HBM = pltpu.MemorySpace.HBM
NT = (((1,), (1,)), ((), ()))


def split3(x):
    hi = x.astype(BF16).astype(F32)
    rest = x - hi
    mid = rest.astype(BF16).astype(F32)
    return hi, mid, rest - mid


def dot(a, b):
    return jnp.dot(a, b, preferred_element_type=F32)


def exact_dot(x, onehot):
    parts = jnp.concatenate([*split3(x), jnp.zeros_like(x)], axis=0)
    r = dot(parts.astype(BF16), onehot)
    return r[0:4] + r[4:8] + r[8:12]


def kernel(
    inv_hbm, src_in, ends_hbm, delay_hbm, admit_hbm, breaker_hbm, hv_hbm, hj_hbm, node_hbm, init_hbm, cap_hbm, count_hbm,
    volt_ref, cap_out, cur_out,
    inv_ref, ends_ref, delay_ref, admit_ref, breaker_ref, hv_ref, hj_ref, node_ref, init_ref, cap_ref, count_ref,
    gt_ref, s_ref, t_ref, q_ref, send1y, buf1y, send1x, buf1x, wsend, wbuf, msg0, buf0, send2y, buf2y, send2x, buf2x, send3, buf3,
    loads, s0, r0, s1y, r1y, s1x, r1x, sw, rw, s2y, r2y, s2x, r2x, s3, r3,
):
    sub, col = lax.axis_index("sub"), lax.axis_index("col")
    y, x = sub // NX, lax.rem(sub, NX)
    z, core = col // 2, lax.rem(col, 2)
    to_y = lambda p: {"sub": p * NX + x}
    to_x = lambda p: {"sub": y * NX + p}
    to_c = lambda p: {"col": p}

    def ring(n, me, to, src, dst, send, recv):
        return [
            (to(p), p, me, src(p), dst, send, recv) for p in [lax.rem(me + d, n) for d in range(1, n)]
        ]

    def copies(exchange):
        return [
            pltpu.make_async_remote_copy(
                src_ref=src, dst_ref=dst.at[there], send_sem=send.at[here], recv_sem=recv.at[there],
                device_id=device, device_id_type=MESH,
            )
            for device, here, there, src, dst, send, recv in exchange
        ]

    def push(exchange):
        for copy in copies(exchange):
            copy.start()

    def await_send(exchange):
        for copy in copies(exchange):
            copy.wait_send()

    def await_recv(exchange):
        for device, here, there, src, dst, send, recv in exchange:
            pltpu.make_async_remote_copy(
                src_ref=src, dst_ref=dst.at[here], send_sem=send.at[here], recv_sem=recv.at[here],
                device_id=device, device_id_type=MESH,
            ).wait_recv()

    fetches = [
        pltpu.make_async_copy(a, b, loads.at[i])
        for i, (a, b) in enumerate(
            [
                (ends_hbm, ends_ref), (node_hbm, node_ref), (inv_hbm, inv_ref), (cap_hbm, cap_ref),
                (count_hbm, count_ref), (init_hbm, init_ref), (delay_hbm, delay_ref), (admit_hbm, admit_ref),
                (breaker_hbm, breaker_ref), (hv_hbm, hv_ref), (hj_hbm, hj_ref),
            ]
        )
    ]
    for fetch in fetches:
        fetch.start()
    barrier = pltpu.get_barrier_semaphore()
    for n, me, to in ((NY, y, to_y), (NX, x, to_x), (NC, col, to_c)):
        for d in range(1, n):
            pl.semaphore_signal(
                barrier, inc=1, device_id=to(lax.rem(me + d, n)), device_id_type=MESH
            )

    lane = lax.broadcasted_iota(jnp.int32, (1, 128), 1)
    row = lax.broadcasted_iota(jnp.int32, (128, 1), 0)
    low = lane < 64
    station_lane = lane < 48
    twice_over = lambda v: jnp.concatenate([v, v], axis=1)

    fetches[0].wait()
    fetches[1].wait()
    e0, e1 = ends_ref[0:1, :], ends_ref[1:2, :]
    flip = e0 >= NS
    ends_row = jnp.concatenate([jnp.where(flip, e1, e0), jnp.where(flip, e0, e1)], axis=1)
    st_row = jnp.concatenate([node_ref[...], jnp.zeros((1, 80), jnp.int32)], axis=1)
    st_row = jnp.where(station_lane, st_row, -1 - lane)
    ends_col = jnp.broadcast_to(ends_row, (128, 128)).T
    st_col = jnp.broadcast_to(st_row, (128, 128)).T
    col192 = jnp.concatenate([ends_col, st_col[0:64]], axis=0)

    place = lax.rem(col192, NS)
    fetches[2].wait()
    acc = jnp.zeros((192, 128), F32)
    for k in range(0, NS, 256):
        halves = [jnp.where(place == lane + (k + h), 1.0, 0.0).astype(BF16) for h in (0, 128)]
        acc += lax.dot_general(
            jnp.concatenate(halves, axis=1), inv_ref[:, k : k + 256], NT, preferred_element_type=F32
        )
    gt = jnp.where((col192 >= NS) == jnp.broadcast_to(lane >= 64, (192, 128)), acc, 0.0)
    gt_ref[...] = gt

    gid = jnp.where(row >= 64, NS - 64, 0) + row + sub * 64
    st_high = pltpu.roll(st_row, 64, 1)
    row0 = jnp.where(low, ends_row, st_high)
    row1 = jnp.where(low, pltpu.roll(ends_row, 64, 1), st_high)
    pick = jnp.where(gid == jnp.where(row >= 64, row1, row0), 1.0, 0.0).astype(BF16)
    piece = lax.rem(z, 6) * 2 + core
    mine = gt_ref[pl.ds(pl.multiple_of(piece * 16, 16), 16), :]
    for c in range(4):
        pair = src_in[c].astype(F32)
        s_ref[c : c + 1, 0:128] = jnp.concatenate([pair[0:1], pair[1:2]], axis=1)
    first_part = [dot(mine.astype(BF16), pick), s_ref[0:4, 0:128], jnp.zeros((12, 128), F32)]
    send1y[...] = jnp.concatenate(first_part, axis=0).astype(BF16)
    pl.semaphore_wait(barrier, NC + NY + NX - 3)

    ex1y = ring(NY, y, to_y, lambda p: send1y, buf1y, s1y, r1y)
    push(ex1y)
    buf1y[y] = send1y[...]

    for i in (3, 4, 5):
        fetches[i].wait()
    position = lax.broadcasted_iota(jnp.int32, (75, 1, 1), 0) + sub * 75
    q_ref[...] = jnp.zeros((40, 128), F32)
    for n in range(STEPS):
        count = count_ref[n]
        part = jnp.sum(jnp.where(position < count[None], cap_ref[...], 0.0), axis=0)
        q_ref[2 * n : 2 * n + 2, 0:96] = part
        q_ref[16 + 2 * n : 18 + 2 * n, 0:96] = count.astype(F32)
    q_ref[32:34, 0:96] = init_ref[...]
    row48 = lax.broadcasted_iota(jnp.int32, (48, 1), 0)
    owner = lane // 4 == row48 // 2
    second = lax.rem(row48, 2) == 1
    moved = jnp.zeros((144, 128), F32)
    for q in range(0, 18, 2):
        wide, fold = [], []
        for h in (q, q + 1):
            v = jnp.where(second, q_ref[2 * h + 1 : 2 * h + 2, :], q_ref[2 * h : 2 * h + 1, :])
            wide.append(jnp.concatenate(split3(jnp.where(owner, v, 0.0)), axis=0).astype(BF16))
            fold.append(jnp.where(lane == 4 * h + lax.rem(row, 4), 1.0, 0.0).astype(BF16))
        moved += dot(jnp.concatenate(wide, axis=1), jnp.concatenate(fold, axis=0))
    moved = moved[0:48] + moved[48:96] + moved[96:144]
    for p in range(NC):
        msg0[p] = moved[2 * p : 2 * p + 2]
    ex0 = ring(NC, col, to_c, lambda p: msg0.at[p], buf0, s0, r0)
    push(ex0)
    buf0[col] = msg0[col]

    await_recv(ex1y)
    parts = [buf1y[p].astype(F32) for p in range(NY)]
    total = parts[0][0:16]
    for part in parts[1:]:
        total += part[0:16]
    send1x[...] = jnp.concatenate([total] + [part[16:20] for part in parts], axis=0).astype(BF16)
    ex1x = ring(NX, x, to_x, lambda p: send1x, buf1x, s1x, r1x)
    push(ex1x)
    buf1x[x] = send1x[...]

    nrow = jnp.concatenate([ends_row, st_row], axis=1)
    ncol = jnp.concatenate([twice_over(ends_col), twice_over(st_col)], axis=0)
    b_row = lax.broadcasted_iota(jnp.int32, (256, 256), 0)
    b_col = lax.broadcasted_iota(jnp.int32, (256, 256), 1)
    equal = ncol == nrow
    earlier = jnp.where(equal & (b_row < b_col), 1.0, 0.0)
    leads = jnp.sum(earlier, axis=0, keepdims=True) == 0.0
    merge = jnp.where(equal & leads, 1.0, 0.0).astype(BF16)
    at_ends = jnp.where(gid == ends_row, 1.0, 0.0).astype(BF16)
    at_st = jnp.where(gid == st_row, 1.0, 0.0).astype(BF16)
    for i in range(6, 11):
        fetches[i].wait()
    delay = twice_over(delay_ref[...])
    twice = 2.0 * twice_over(admit_ref[...])
    in_service = twice_over(breaker_ref[...].astype(F32))
    flips = twice_over(jnp.where(flip, 1, 0))
    end_of = 2 * jnp.where(low, lane, lane - 64) + jnp.where(low, flips, 1 - flips)
    perm = jnp.where(row == end_of, 1.0, 0.0).astype(BF16)
    hist = jnp.concatenate([hv_ref[t] for t in range(DMAX)] + [hj_ref[t] for t in range(DMAX)], axis=0)
    hist = dot(jnp.concatenate(split3(hist), axis=0).astype(BF16), perm)
    hist = hist[0:48] + hist[48:96] + hist[96:144]
    volts = [hist[4 * t : 4 * t + 4] for t in range(DMAX)]
    injs = [hist[24 + 4 * t : 28 + 4 * t] for t in range(DMAX)]

    await_recv(ex1x)
    parts = [buf1x[p].astype(F32) for p in range(NX)]
    block = parts[0][0:16]
    for part in parts[1:]:
        block += part[0:16]
    wsend[...] = block.astype(BF16)
    exw = []
    for dz in (1, -1, 2, -2, 3, 0):
        for dk in (0, 1):
            if dz or dk:
                k_to = lax.rem(core + dk, 2)
                z_to, z_from = lax.rem(z + dz + 12, 12), lax.rem(z - dz + 12, 12)
                exw.append(
                    ({"col": z_to * 2 + k_to}, lax.rem(z_from, 6) * 2 + k_to, piece, wsend, wbuf, sw, rw)
                )
    push(exw)
    wbuf[piece] = wsend[...]
    for p in range(NY):
        for q in range(NX // 2):
            a = parts[2 * q][16 + 4 * p : 20 + 4 * p]
            b = parts[2 * q + 1][16 + 4 * p : 20 + 4 * p]
            m = (2 * p + q) * 128
            s_ref[0:4, m : m + 128] = jnp.where(low, a, pltpu.roll(b, 64, 1))
            s_ref[4:8, m : m + 128] = jnp.where(low, pltpu.roll(a, 64, 1), b)
    both = lax.dot_general(s_ref[...].astype(BF16), inv_ref[...], NT, preferred_element_type=F32)
    source_part = jnp.where(low, both[0:4], both[4:8])
    send2y[16:20, :] = exact_dot(source_part, at_ends)
    send2y[20:24, :] = exact_dot(source_part, at_st)

    await_recv(ex0)
    t_ref[...] = jnp.zeros((128, 128), F32)
    for p in range(NC):
        t_ref[2 * p : 2 * p + 2, :] = buf0[p]
    stations = t_ref[...].T
    send2y[0:16, :] = jnp.where(low, stations[0:16], pltpu.roll(stations[16:32], 64, 1))
    ex2y = ring(NY, y, to_y, lambda p: send2y, buf2y, s2y, r2y)
    push(ex2y)
    buf2y[y] = send2y[...]

    await_recv(exw)
    w = jnp.concatenate([wbuf[p].astype(F32) for p in range(12)], axis=0)
    high_w = pltpu.roll(w, 64, 1)
    is_high = col192 >= NS
    w_ends = jnp.where(low, jnp.where(is_high, 0.0, w), jnp.where(is_high, high_w, 0.0))
    w_st = jnp.where(low, high_w, 0.0)
    w_full = jnp.concatenate(
        [jnp.concatenate([w_ends, w_st], axis=1), jnp.zeros((64, 256), F32)], axis=0
    ).astype(BF16)

    await_recv(ex2y)
    total = buf2y[0]
    for p in range(1, NY):
        total += buf2y[p]
    send2x[...] = total
    ex2x = ring(NX, x, to_x, lambda p: send2x, buf2x, s2x, r2x)
    push(ex2x)
    buf2x[x] = total

    await_recv(ex2x)
    total = buf2x[0]
    for p in range(1, NX):
        total += buf2x[p]
    sums = jnp.where(
        station_lane,
        jnp.concatenate([total[0:16], pltpu.roll(total[0:16], 64, 1)], axis=0),
        0.0,
    )
    src_nodes = jnp.concatenate([total[16:20], total[20:24]], axis=1)

    counts = [jnp.where(station_lane, stations[32 + 4 * n : 36 + 4 * n], 0.0) for n in range(STEPS)]
    node_volt = jnp.where(station_lane, stations[64:68], 0.0)
    currents = []
    for n in range(STEPS):
        u, j = volts[n + DMAX - DMIN], injs[n + DMAX - DMIN]
        for d in range(DMIN + 1, DMAX + 1):
            u = jnp.where(delay == d, volts[n + DMAX - d], u)
            j = jnp.where(delay == d, injs[n + DMAX - d], j)
        injection = in_service * (twice * pltpu.roll(u, 64, 1) - pltpu.roll(j, 64, 1))
        injs.append(injection)
        charge = sums[4 * n : 4 * n + 4]
        for q in range(n):
            charge -= 0.5 * jnp.minimum(counts[n], counts[q]) * currents[q]
        current = (2.0 / SM * charge - node_volt) / (1.0 + counts[n] / SM)
        current = jnp.where(station_lane, current, 0.0)
        currents.append(current)
        term = exact_dot(jnp.concatenate([injection, current], axis=1), merge)
        term = jnp.concatenate([term, jnp.zeros_like(term)], axis=0).astype(BF16)
        if n + 1 < STEPS:
            nodes = dot(term, w_full)[0:4] + src_nodes
            volts.append(nodes[:, 0:128])
            node_volt = nodes[:, 128:256]

    t_ref[0:32, :] = jnp.concatenate(currents, axis=0)
    t_ref[32:128, :] = jnp.zeros((96, 128), F32)
    out = t_ref[...].T
    for p in range(NC):
        send3[p] = out[2 * p : 2 * p + 2, :]
    ex3 = ring(NC, col, to_c, lambda p: send3.at[p], buf3, s3, r3)
    push(ex3)
    buf3[col] = send3[col]
    last = dot(term, jnp.concatenate([gt, jnp.zeros((64, 128), F32)], axis=0).astype(BF16))
    final = source_part + last[0:4]
    for c in range(4):
        volt_ref[c] = jnp.concatenate([final[c : c + 1, 0:64], final[c : c + 1, 64:128]], axis=0)
    spread = [jnp.where(row == 4 * n + lax.rem(lane, 4), 1.0, 0.0).astype(BF16) for n in range(STEPS)]
    spread = jnp.concatenate(spread, axis=1)
    for ex in (ex0, ex1y, ex1x, exw, ex2y, ex2x):
        await_send(ex)
    await_recv(ex3)
    for p in range(NC):
        t_ref[2 * p : 2 * p + 2, :] = buf3[p]
    wide = dot(jnp.concatenate(split3(t_ref[0:48, :]), axis=0).astype(BF16), spread)
    wide = wide[0:48] + wide[48:96] + wide[96:144]
    discharge = jnp.zeros((75, 2, 96), F32)
    for n in range(STEPS):
        tile = jnp.where(owner, wide[:, 128 * n : 128 * n + 128], 0.0)
        rows = [jnp.sum(jnp.where(second == s, tile, 0.0), axis=0, keepdims=True) for s in (False, True)]
        current = jnp.concatenate(rows, axis=0)[:, 0:96]
        cur_out[n] = current
        discharge += jnp.where(position < count_ref[n][None], current[None], 0.0)
    cap_out[...] = cap_ref[...] - 0.5 * discharge
    await_send(ex3)


def write_kernel(a, b, c, x, y, z, sems):
    copies = [pltpu.make_async_copy(s, d, sems.at[i]) for i, (s, d) in enumerate(((a, x), (b, y), (c, z)))]
    for copy in copies:
        copy.start()
    for copy in copies:
        copy.wait()


def exchange(*inputs):
    vmem, hbm = pl.BlockSpec(memory_space=pltpu.VMEM), pl.BlockSpec(memory_space=HBM)
    pairs = lambda n: [pltpu.SemaphoreType.DMA((n,)), pltpu.SemaphoreType.DMA((n,))]
    outs = tuple(jax.ShapeDtypeStruct(s, F32) for s in ((4, 2, 64), (75, 2, 96), (STEPS, 2, 96)))
    fetched = [inputs[0]] + list(inputs[2:])
    results = pl.pallas_call(
        kernel,
        out_shape=outs,
        in_specs=[hbm, vmem] + [hbm] * 10,
        out_specs=(vmem,) * 3,
        scratch_shapes=[
            *(pltpu.VMEM(v.shape, v.dtype) for v in fetched),
            pltpu.VMEM((192, 128), F32),
            pltpu.VMEM((8, NS), F32),
            pltpu.VMEM((128, 128), F32),
            pltpu.VMEM((40, 128), F32),
            pltpu.VMEM((32, 128), BF16),
            pltpu.VMEM((NY, 32, 128), BF16),
            pltpu.VMEM((48, 128), BF16),
            pltpu.VMEM((NX, 48, 128), BF16),
            pltpu.VMEM((16, 128), BF16),
            pltpu.VMEM((12, 16, 128), BF16),
            pltpu.VMEM((NC, 2, 128), F32),
            pltpu.VMEM((NC, 2, 128), F32),
            pltpu.VMEM((24, 128), F32),
            pltpu.VMEM((NY, 24, 128), F32),
            pltpu.VMEM((24, 128), F32),
            pltpu.VMEM((NX, 24, 128), F32),
            pltpu.VMEM((NC, 2, 128), F32),
            pltpu.VMEM((NC, 2, 128), F32),
            pltpu.SemaphoreType.DMA((11,)),
            *pairs(NC), *pairs(NY), *pairs(NX), *pairs(12), *pairs(NY), *pairs(NX), *pairs(NC),
        ],
        compiler_params=pltpu.CompilerParams(
            collective_id=0, has_side_effects=True, vmem_limit_bytes=60 * 1024 * 1024
        ),
    )(*inputs)
    return pl.pallas_call(
        write_kernel,
        out_shape=outs,
        in_specs=[vmem] * 3,
        out_specs=(hbm,) * 3,
        scratch_shapes=[pltpu.SemaphoreType.DMA((3,))],
        compiler_params=pltpu.CompilerParams(vmem_limit_bytes=60 * 1024 * 1024),
    )(*results)


def per_device(
    inv_conductance, source, line_ends, delays, admittance, breaker, hist_volt, hist_inj,
    station_node, station_initial, capacitor_initial, insert_count,
):
    volts, capacitor, current = exchange(
        inv_conductance.reshape(128, NS), source, line_ends.T, delays[None, :], admittance[None, :],
        breaker.T, hist_volt, hist_inj, station_node[None, :], station_initial.T,
        capacitor_initial.transpose(2, 1, 0), insert_count.transpose(0, 2, 1),
    )
    return volts, capacitor.transpose(2, 1, 0), current.transpose(0, 2, 1)


def solution(mesh):
    in_specs = (
        P(None, "sub", None),
        P("col", None, "sub"),
        P(),
        P(),
        P(),
        P(None, "col"),
        P(None, "col", None),
        P(None, "col", None),
        P(),
        P(None, "col"),
        P(None, "col", "sub"),
        P(None, None, "col"),
    )
    out_specs = (P("col", None, "sub"), P(None, "col", "sub"), P(None, None, "col"))
    return jax.shard_map(
        per_device, mesh=mesh, in_specs=in_specs, out_specs=out_specs, check_vma=False
    )
```

```python
import jax
import jax.numpy as jnp
from jax import lax
from jax.experimental import pallas as pl
from jax.experimental.pallas import tpu as pltpu
from jax.sharding import PartitionSpec as P

SM = 2400
STEPS = 8
DMIN = 2
DMAX = 6
NS = 2048
NX, NY, NC = 4, 8, 24
F32, BF16 = jnp.float32, jnp.bfloat16
MESH = pl.DeviceIdType.MESH
HBM = pltpu.MemorySpace.HBM
NT = (((1,), (1,)), ((), ()))


def split3(x):
    hi = x.astype(BF16).astype(F32)
    rest = x - hi
    mid = rest.astype(BF16).astype(F32)
    return hi, mid, rest - mid


def dot(a, b):
    return jnp.dot(a, b, preferred_element_type=F32)


def exact_dot(x, onehot):
    parts = jnp.concatenate([*split3(x), jnp.zeros_like(x)], axis=0)
    r = dot(parts.astype(BF16), onehot)
    return r[0:4] + r[4:8] + r[8:12]


def kernel(
    inv_hbm, src_in, ends_hbm, delay_hbm, admit_hbm, breaker_hbm, hv_hbm, hj_hbm, node_hbm, init_hbm, cap_hbm, count_hbm,
    volt_ref, cap_out, cur_out,
    inv_ref, ends_ref, delay_ref, admit_ref, breaker_ref, hv_ref, hj_ref, node_ref, init_ref, cap_ref, count_ref,
    gt_ref, s_ref, t_ref, q_ref, sends, bufs, send1y, buf1y, send1x, buf1x, wsend, wbuf, msg0, buf0, send2y, buf2y, send2x, buf2x, send3, buf3,
    loads, s0, r0, ss, rs, s1y, r1y, s1x, r1x, sw, rw, s2y, r2y, s2x, r2x, s3, r3,
):
    sub, col = lax.axis_index("sub"), lax.axis_index("col")
    y, x = sub // NX, lax.rem(sub, NX)
    z, core = col // 2, lax.rem(col, 2)
    to_y = lambda p: {"sub": p * NX + x}
    to_x = lambda p: {"sub": y * NX + p}
    to_c = lambda p: {"col": p}

    far = lambda n: sorted(range(1, n), key=lambda d: -min(d, n - d))

    def ring(n, me, to, src, dst, send, recv):
        return [(to(p), p, me, src(p), dst, send, recv) for p in [lax.rem(me + d, n) for d in far(n)]]

    def plane(src, dst, send, recv):
        offsets = sorted(
            [(dy, dx) for dy in range(NY) for dx in range(NX) if dy or dx],
            key=lambda o: -(min(o[0], NY - o[0]) + min(o[1], NX - o[1])),
        )
        peers = [lax.rem(y + dy, NY) * NX + lax.rem(x + dx, NX) for dy, dx in offsets]
        return [({"sub": p}, p, sub, src, dst, send, recv) for p in peers]

    def copies(exchange):
        return [
            pltpu.make_async_remote_copy(
                src_ref=src, dst_ref=dst.at[there], send_sem=send.at[here], recv_sem=recv.at[there],
                device_id=device, device_id_type=MESH,
            )
            for device, here, there, src, dst, send, recv in exchange
        ]

    def push(exchange):
        for copy in copies(exchange):
            copy.start()

    def await_send(exchange):
        for copy in copies(exchange):
            copy.wait_send()

    def await_recv(exchange):
        for device, here, there, src, dst, send, recv in exchange:
            pltpu.make_async_remote_copy(
                src_ref=src, dst_ref=dst.at[here], send_sem=send.at[here], recv_sem=recv.at[here],
                device_id=device, device_id_type=MESH,
            ).wait_recv()

    fetches = [
        pltpu.make_async_copy(a, b, loads.at[i])
        for i, (a, b) in enumerate(
            [
                (ends_hbm, ends_ref), (node_hbm, node_ref), (inv_hbm, inv_ref), (cap_hbm, cap_ref),
                (count_hbm, count_ref), (init_hbm, init_ref), (delay_hbm, delay_ref), (admit_hbm, admit_ref),
                (breaker_hbm, breaker_ref), (hv_hbm, hv_ref), (hj_hbm, hj_ref),
            ]
        )
    ]
    for fetch in fetches:
        fetch.start()
    barrier = pltpu.get_barrier_semaphore()
    greeted = [to_c(lax.rem(col + d, NC)) for d in far(NC)]
    greeted += [peer[0] for peer in plane(None, None, None, None)]
    for device in greeted:
        pl.semaphore_signal(barrier, inc=1, device_id=device, device_id_type=MESH)

    lane = lax.broadcasted_iota(jnp.int32, (1, 128), 1)
    row = lax.broadcasted_iota(jnp.int32, (128, 1), 0)
    low = lane < 64
    station_lane = lane < 48
    twice_over = lambda v: jnp.concatenate([v, v], axis=1)

    for i in (3, 4, 5):
        fetches[i].wait()
    position = lax.broadcasted_iota(jnp.int32, (75, 1, 1), 0) + sub * 75
    q_ref[...] = jnp.zeros((40, 128), F32)
    for n in range(STEPS):
        count = count_ref[n]
        part = jnp.sum(jnp.where(position < count[None], cap_ref[...], 0.0), axis=0)
        q_ref[2 * n : 2 * n + 2, 0:96] = part
        q_ref[16 + 2 * n : 18 + 2 * n, 0:96] = count.astype(F32)
    q_ref[32:34, 0:96] = init_ref[...]
    row48 = lax.broadcasted_iota(jnp.int32, (48, 1), 0)
    owner = lane // 4 == row48 // 2
    second = lax.rem(row48, 2) == 1
    moved = jnp.zeros((144, 128), F32)
    for q in range(0, 18, 2):
        wide, fold = [], []
        for h in (q, q + 1):
            v = jnp.where(second, q_ref[2 * h + 1 : 2 * h + 2, :], q_ref[2 * h : 2 * h + 1, :])
            wide.append(jnp.concatenate(split3(jnp.where(owner, v, 0.0)), axis=0).astype(BF16))
            fold.append(jnp.where(lane == 4 * h + lax.rem(row, 4), 1.0, 0.0).astype(BF16))
        moved += dot(jnp.concatenate(wide, axis=1), jnp.concatenate(fold, axis=0))
    moved = moved[0:48] + moved[48:96] + moved[96:144]
    for p in range(NC):
        msg0[p] = moved[2 * p : 2 * p + 2]
    for c in range(4):
        pair = src_in[c].astype(F32)
        sends[c : c + 1, :] = jnp.concatenate([pair[0:1], pair[1:2]], axis=1)
    pl.semaphore_wait(barrier, NC + NX * NY - 2)
    ex0 = ring(NC, col, to_c, lambda p: msg0.at[p], buf0, s0, r0)
    push(ex0)
    buf0[col] = msg0[col]

    exs = plane(sends, bufs, ss, rs)
    push(exs)
    bufs[sub] = sends[...]

    fetches[0].wait()
    fetches[1].wait()
    e0, e1 = ends_ref[0:1, :], ends_ref[1:2, :]
    flip = e0 >= NS
    ends_row = jnp.concatenate([jnp.where(flip, e1, e0), jnp.where(flip, e0, e1)], axis=1)
    st_row = jnp.concatenate([node_ref[...], jnp.zeros((1, 80), jnp.int32)], axis=1)
    st_row = jnp.where(station_lane, st_row, -1 - lane)
    ends_col = jnp.broadcast_to(ends_row, (128, 128)).T
    st_col = jnp.broadcast_to(st_row, (128, 128)).T
    col192 = jnp.concatenate([ends_col, st_col[0:64]], axis=0)

    place = lax.rem(col192, NS)
    fetches[2].wait()
    acc = jnp.zeros((192, 128), F32)
    for k in range(0, NS, 256):
        halves = [jnp.where(place == lane + (k + h), 1.0, 0.0).astype(BF16) for h in (0, 128)]
        acc += lax.dot_general(
            jnp.concatenate(halves, axis=1), inv_ref[:, k : k + 256], NT, preferred_element_type=F32
        )
    gt = jnp.where((col192 >= NS) == jnp.broadcast_to(lane >= 64, (192, 128)), acc, 0.0)
    gt_ref[...] = gt

    gid = jnp.where(row >= 64, NS - 64, 0) + row + sub * 64
    st_high = pltpu.roll(st_row, 64, 1)
    row0 = jnp.where(low, ends_row, st_high)
    row1 = jnp.where(low, pltpu.roll(ends_row, 64, 1), st_high)
    pick = jnp.where(gid == jnp.where(row >= 64, row1, row0), 1.0, 0.0).astype(BF16)
    piece = lax.rem(z, 6) * 2 + core
    mine = gt_ref[pl.ds(pl.multiple_of(piece * 16, 16), 16), :]
    send1y[...] = dot(mine.astype(BF16), pick).astype(BF16)

    ex1y = ring(NY, y, to_y, lambda p: send1y, buf1y, s1y, r1y)
    push(ex1y)
    buf1y[y] = send1y[...]

    nrow = jnp.concatenate([ends_row, st_row], axis=1)
    ncol = jnp.concatenate([twice_over(ends_col), twice_over(st_col)], axis=0)
    b_row = lax.broadcasted_iota(jnp.int32, (256, 256), 0)
    b_col = lax.broadcasted_iota(jnp.int32, (256, 256), 1)
    equal = ncol == nrow
    earlier = jnp.where(equal & (b_row < b_col), 1.0, 0.0)
    leads = jnp.sum(earlier, axis=0, keepdims=True) == 0.0
    merge = jnp.where(equal & leads, 1.0, 0.0).astype(BF16)
    at_ends = jnp.where(gid == ends_row, 1.0, 0.0).astype(BF16)
    at_st = jnp.where(gid == st_row, 1.0, 0.0).astype(BF16)
    for i in range(6, 11):
        fetches[i].wait()
    delay = twice_over(delay_ref[...])
    twice = 2.0 * twice_over(admit_ref[...])
    in_service = twice_over(breaker_ref[...].astype(F32))
    flips = twice_over(jnp.where(flip, 1, 0))
    end_of = 2 * jnp.where(low, lane, lane - 64) + jnp.where(low, flips, 1 - flips)
    perm = jnp.where(row == end_of, 1.0, 0.0).astype(BF16)
    hist = jnp.concatenate([hv_ref[t] for t in range(DMAX)] + [hj_ref[t] for t in range(DMAX)], axis=0)
    hist = dot(jnp.concatenate(split3(hist), axis=0).astype(BF16), perm)
    hist = hist[0:48] + hist[48:96] + hist[96:144]
    volts = [hist[4 * t : 4 * t + 4] for t in range(DMAX)]
    injs = [hist[24 + 4 * t : 28 + 4 * t] for t in range(DMAX)]

    await_recv(exs)
    for p in range(NY):
        for q in range(NX // 2):
            a = bufs[4 * p + 2 * q]
            b = bufs[4 * p + 2 * q + 1]
            m = (2 * p + q) * 128
            s_ref[0:4, m : m + 128] = jnp.where(low, a, pltpu.roll(b, 64, 1))
            s_ref[4:8, m : m + 128] = jnp.where(low, pltpu.roll(a, 64, 1), b)
    both = lax.dot_general(s_ref[...].astype(BF16), inv_ref[...], NT, preferred_element_type=F32)
    source_part = jnp.where(low, both[0:4], both[4:8])
    send2y[16:20, :] = exact_dot(source_part, at_ends)
    send2y[20:24, :] = exact_dot(source_part, at_st)

    await_recv(ex0)
    t_ref[...] = jnp.zeros((128, 128), F32)
    for p in range(NC):
        t_ref[2 * p : 2 * p + 2, :] = buf0[p]
    stations = t_ref[...].T
    send2y[0:16, :] = jnp.where(low, stations[0:16], pltpu.roll(stations[16:32], 64, 1))
    ex2y = ring(NY, y, to_y, lambda p: send2y, buf2y, s2y, r2y)
    push(ex2y)
    buf2y[y] = send2y[...]

    await_recv(ex1y)
    parts = [buf1y[p].astype(F32) for p in range(NY)]
    total = parts[0]
    for part in parts[1:]:
        total += part
    send1x[...] = total.astype(BF16)
    ex1x = ring(NX, x, to_x, lambda p: send1x, buf1x, s1x, r1x)
    push(ex1x)
    buf1x[x] = send1x[...]

    await_recv(ex1x)
    parts = [buf1x[p].astype(F32) for p in range(NX)]
    block = parts[0]
    for part in parts[1:]:
        block += part
    wsend[...] = block.astype(BF16)
    exw = []
    for dz in (1, -1, 2, -2, 3, 0):
        for dk in (0, 1):
            if dz or dk:
                k_to = lax.rem(core + dk, 2)
                z_to, z_from = lax.rem(z + dz + 12, 12), lax.rem(z - dz + 12, 12)
                exw.append(
                    ({"col": z_to * 2 + k_to}, lax.rem(z_from, 6) * 2 + k_to, piece, wsend, wbuf, sw, rw)
                )
    push(exw)
    wbuf[piece] = wsend[...]

    await_recv(ex2y)
    total = buf2y[0]
    for p in range(1, NY):
        total += buf2y[p]
    send2x[...] = total
    ex2x = ring(NX, x, to_x, lambda p: send2x, buf2x, s2x, r2x)
    push(ex2x)
    buf2x[x] = total

    await_recv(exw)
    w = jnp.concatenate([wbuf[p].astype(F32) for p in range(12)], axis=0)
    high_w = pltpu.roll(w, 64, 1)
    is_high = col192 >= NS
    w_ends = jnp.where(low, jnp.where(is_high, 0.0, w), jnp.where(is_high, high_w, 0.0))
    w_st = jnp.where(low, high_w, 0.0)
    w_full = jnp.concatenate(
        [jnp.concatenate([w_ends, w_st], axis=1), jnp.zeros((64, 256), F32)], axis=0
    ).astype(BF16)

    await_recv(ex2x)
    total = buf2x[0]
    for p in range(1, NX):
        total += buf2x[p]
    sums = jnp.where(
        station_lane,
        jnp.concatenate([total[0:16], pltpu.roll(total[0:16], 64, 1)], axis=0),
        0.0,
    )
    src_nodes = jnp.concatenate([total[16:20], total[20:24]], axis=1)

    counts = [jnp.where(station_lane, stations[32 + 4 * n : 36 + 4 * n], 0.0) for n in range(STEPS)]
    node_volt = jnp.where(station_lane, stations[64:68], 0.0)
    currents = []
    for n in range(STEPS):
        u, j = volts[n + DMAX - DMIN], injs[n + DMAX - DMIN]
        for d in range(DMIN + 1, DMAX + 1):
            u = jnp.where(delay == d, volts[n + DMAX - d], u)
            j = jnp.where(delay == d, injs[n + DMAX - d], j)
        injection = in_service * (twice * pltpu.roll(u, 64, 1) - pltpu.roll(j, 64, 1))
        injs.append(injection)
        charge = sums[4 * n : 4 * n + 4]
        for q in range(n):
            charge -= 0.5 * jnp.minimum(counts[n], counts[q]) * currents[q]
        current = (2.0 / SM * charge - node_volt) / (1.0 + counts[n] / SM)
        current = jnp.where(station_lane, current, 0.0)
        currents.append(current)
        term = exact_dot(jnp.concatenate([injection, current], axis=1), merge)
        term = jnp.concatenate([term, jnp.zeros_like(term)], axis=0).astype(BF16)
        if n + 1 < STEPS:
            nodes = dot(term, w_full)[0:4] + src_nodes
            volts.append(nodes[:, 0:128])
            node_volt = nodes[:, 128:256]

    t_ref[0:32, :] = jnp.concatenate(currents, axis=0)
    t_ref[32:128, :] = jnp.zeros((96, 128), F32)
    out = t_ref[...].T
    for p in range(NC):
        send3[p] = out[2 * p : 2 * p + 2, :]
    ex3 = ring(NC, col, to_c, lambda p: send3.at[p], buf3, s3, r3)
    push(ex3)
    buf3[col] = send3[col]
    last = dot(term, jnp.concatenate([gt, jnp.zeros((64, 128), F32)], axis=0).astype(BF16))
    final = source_part + last[0:4]
    for c in range(4):
        volt_ref[c] = jnp.concatenate([final[c : c + 1, 0:64], final[c : c + 1, 64:128]], axis=0)
    spread = [jnp.where(row == 4 * n + lax.rem(lane, 4), 1.0, 0.0).astype(BF16) for n in range(STEPS)]
    spread = jnp.concatenate(spread, axis=1)
    for ex in (ex0, exs, ex1y, ex1x, exw, ex2y, ex2x):
        await_send(ex)
    await_recv(ex3)
    for p in range(NC):
        t_ref[2 * p : 2 * p + 2, :] = buf3[p]
    wide = dot(jnp.concatenate(split3(t_ref[0:48, :]), axis=0).astype(BF16), spread)
    wide = wide[0:48] + wide[48:96] + wide[96:144]
    discharge = jnp.zeros((75, 2, 96), F32)
    for n in range(STEPS):
        tile = jnp.where(owner, wide[:, 128 * n : 128 * n + 128], 0.0)
        rows = [jnp.sum(jnp.where(second == s, tile, 0.0), axis=0, keepdims=True) for s in (False, True)]
        current = jnp.concatenate(rows, axis=0)[:, 0:96]
        cur_out[n] = current
        discharge += jnp.where(position < count_ref[n][None], current[None], 0.0)
    cap_out[...] = cap_ref[...] - 0.5 * discharge
    await_send(ex3)


def write_kernel(a, b, c, x, y, z, sems):
    copies = [pltpu.make_async_copy(s, d, sems.at[i]) for i, (s, d) in enumerate(((a, x), (b, y), (c, z)))]
    for copy in copies:
        copy.start()
    for copy in copies:
        copy.wait()


def exchange(*inputs):
    vmem, hbm = pl.BlockSpec(memory_space=pltpu.VMEM), pl.BlockSpec(memory_space=HBM)
    pairs = lambda n: [pltpu.SemaphoreType.DMA((n,)), pltpu.SemaphoreType.DMA((n,))]
    outs = tuple(jax.ShapeDtypeStruct(s, F32) for s in ((4, 2, 64), (75, 2, 96), (STEPS, 2, 96)))
    fetched = [inputs[0]] + list(inputs[2:])
    results = pl.pallas_call(
        kernel,
        out_shape=outs,
        in_specs=[hbm, vmem] + [hbm] * 10,
        out_specs=(vmem,) * 3,
        scratch_shapes=[
            *(pltpu.VMEM(v.shape, v.dtype) for v in fetched),
            pltpu.VMEM((192, 128), F32),
            pltpu.VMEM((8, NS), F32),
            pltpu.VMEM((128, 128), F32),
            pltpu.VMEM((40, 128), F32),
            pltpu.VMEM((4, 128), F32),
            pltpu.VMEM((NX * NY, 4, 128), F32),
            pltpu.VMEM((16, 128), BF16),
            pltpu.VMEM((NY, 16, 128), BF16),
            pltpu.VMEM((16, 128), BF16),
            pltpu.VMEM((NX, 16, 128), BF16),
            pltpu.VMEM((16, 128), BF16),
            pltpu.VMEM((12, 16, 128), BF16),
            pltpu.VMEM((NC, 2, 128), F32),
            pltpu.VMEM((NC, 2, 128), F32),
            pltpu.VMEM((24, 128), F32),
            pltpu.VMEM((NY, 24, 128), F32),
            pltpu.VMEM((24, 128), F32),
            pltpu.VMEM((NX, 24, 128), F32),
            pltpu.VMEM((NC, 2, 128), F32),
            pltpu.VMEM((NC, 2, 128), F32),
            pltpu.SemaphoreType.DMA((11,)),
            *pairs(NC), *pairs(NX * NY), *pairs(NY), *pairs(NX), *pairs(12), *pairs(NY), *pairs(NX), *pairs(NC),
        ],
        compiler_params=pltpu.CompilerParams(
            collective_id=0, has_side_effects=True, vmem_limit_bytes=60 * 1024 * 1024
        ),
    )(*inputs)
    return pl.pallas_call(
        write_kernel,
        out_shape=outs,
        in_specs=[vmem] * 3,
        out_specs=(hbm,) * 3,
        scratch_shapes=[pltpu.SemaphoreType.DMA((3,))],
        compiler_params=pltpu.CompilerParams(vmem_limit_bytes=60 * 1024 * 1024),
    )(*results)


def per_device(
    inv_conductance, source, line_ends, delays, admittance, breaker, hist_volt, hist_inj,
    station_node, station_initial, capacitor_initial, insert_count,
):
    volts, capacitor, current = exchange(
        inv_conductance.reshape(128, NS), source, line_ends.T, delays[None, :], admittance[None, :],
        breaker.T, hist_volt, hist_inj, station_node[None, :], station_initial.T,
        capacitor_initial.transpose(2, 1, 0), insert_count.transpose(0, 2, 1),
    )
    return volts, capacitor.transpose(2, 1, 0), current.transpose(0, 2, 1)


def solution(mesh):
    in_specs = (
        P(None, "sub", None),
        P("col", None, "sub"),
        P(),
        P(),
        P(),
        P(None, "col"),
        P(None, "col", None),
        P(None, "col", None),
        P(),
        P(None, "col"),
        P(None, "col", "sub"),
        P(None, None, "col"),
    )
    out_specs = (P("col", None, "sub"), P(None, "col", "sub"), P(None, None, "col"))
    return jax.shard_map(
        per_device, mesh=mesh, in_specs=in_specs, out_specs=out_specs, check_vma=False
    )
```

```python
import jax
import jax.numpy as jnp
from jax import lax
from jax.experimental import pallas as pl
from jax.experimental.pallas import tpu as pltpu
from jax.sharding import PartitionSpec as P

SM = 2400
STEPS = 8
DMIN = 2
DMAX = 6
NS = 2048
NX, NY, NC = 4, 8, 24
F32, BF16 = jnp.float32, jnp.bfloat16
MESH = pl.DeviceIdType.MESH
HBM = pltpu.MemorySpace.HBM
NT = (((1,), (1,)), ((), ()))


def split3(x):
    hi = x.astype(BF16).astype(F32)
    rest = x - hi
    mid = rest.astype(BF16).astype(F32)
    return hi, mid, rest - mid


def dot(a, b):
    return jnp.dot(a, b, preferred_element_type=F32)


def exact_dot(x, onehot):
    parts = jnp.concatenate([*split3(x), jnp.zeros_like(x)], axis=0)
    r = dot(parts.astype(BF16), onehot)
    return r[0:4] + r[4:8] + r[8:12]


def kernel(
    inv_hbm, src_in, ends_hbm, delay_hbm, admit_hbm, breaker_hbm, hv_hbm, hj_hbm, node_hbm, init_hbm, cap_hbm, count_hbm,
    volt_ref, cap_out, cur_out,
    inv_ref, ends_ref, delay_ref, admit_ref, breaker_ref, hv_ref, hj_ref, node_ref, init_ref, cap_ref, count_ref,
    gt_ref, s_ref, t_ref, q_ref, sends, bufs, send1y, buf1y, send1x, buf1x, wsend, wbuf, msg0, buf0, send2y, buf2y, send2x, buf2x, send3, buf3,
    loads, s0, r0, ss, rs, s1y, r1y, s1x, r1x, sw, rw, s2y, r2y, s2x, r2x, s3, r3,
):
    sub, col = lax.axis_index("sub"), lax.axis_index("col")
    y, x = sub // NX, lax.rem(sub, NX)
    z, core = col // 2, lax.rem(col, 2)
    to_y = lambda p: {"sub": p * NX + x}
    to_x = lambda p: {"sub": y * NX + p}
    to_c = lambda p: {"col": p}

    far = lambda n: sorted(range(1, n), key=lambda d: -min(d, n - d))

    def ring(n, me, to, src, dst, send, recv):
        return [(to(p), p, me, src(p), dst, send, recv) for p in [lax.rem(me + d, n) for d in far(n)]]

    def plane(src, dst, send, recv):
        offsets = sorted(
            [(dy, dx) for dy in range(NY) for dx in range(NX) if dy or dx],
            key=lambda o: -(min(o[0], NY - o[0]) + min(o[1], NX - o[1])),
        )
        peers = [lax.rem(y + dy, NY) * NX + lax.rem(x + dx, NX) for dy, dx in offsets]
        return [({"sub": p}, p, sub, src, dst, send, recv) for p in peers]

    def copies(exchange):
        return [
            pltpu.make_async_remote_copy(
                src_ref=src, dst_ref=dst.at[there], send_sem=send.at[here], recv_sem=recv.at[there],
                device_id=device, device_id_type=MESH,
            )
            for device, here, there, src, dst, send, recv in exchange
        ]

    def push(exchange):
        for copy in copies(exchange):
            copy.start()

    def await_send(exchange):
        for copy in copies(exchange):
            copy.wait_send()

    def await_recv(exchange):
        for device, here, there, src, dst, send, recv in exchange:
            pltpu.make_async_remote_copy(
                src_ref=src, dst_ref=dst.at[here], send_sem=send.at[here], recv_sem=recv.at[here],
                device_id=device, device_id_type=MESH,
            ).wait_recv()

    fetches = [
        pltpu.make_async_copy(a, b, loads.at[i])
        for i, (a, b) in enumerate(
            [
                (ends_hbm, ends_ref), (node_hbm, node_ref), (inv_hbm, inv_ref), (cap_hbm, cap_ref),
                (count_hbm, count_ref), (init_hbm, init_ref), (delay_hbm, delay_ref), (admit_hbm, admit_ref),
                (breaker_hbm, breaker_ref), (hv_hbm, hv_ref), (hj_hbm, hj_ref),
            ]
        )
    ]
    for fetch in fetches:
        fetch.start()
    barrier = pltpu.get_barrier_semaphore()
    greeted = [to_c(lax.rem(col + d, NC)) for d in far(NC)]
    greeted += [peer[0] for peer in plane(None, None, None, None)]
    for device in greeted:
        pl.semaphore_signal(barrier, inc=1, device_id=device, device_id_type=MESH)

    lane = lax.broadcasted_iota(jnp.int32, (1, 128), 1)
    row = lax.broadcasted_iota(jnp.int32, (128, 1), 0)
    low = lane < 64
    station_lane = lane < 48
    twice_over = lambda v: jnp.concatenate([v, v], axis=1)

    for i in (3, 4, 5):
        fetches[i].wait()
    position = lax.broadcasted_iota(jnp.int32, (75, 1, 1), 0) + sub * 75
    q_ref[...] = jnp.zeros((40, 128), F32)
    for n in range(STEPS):
        count = count_ref[n]
        part = jnp.sum(jnp.where(position < count[None], cap_ref[...], 0.0), axis=0)
        q_ref[2 * n : 2 * n + 2, 0:96] = part
        q_ref[16 + 2 * n : 18 + 2 * n, 0:96] = count.astype(F32)
    q_ref[32:34, 0:96] = init_ref[...]
    row48 = lax.broadcasted_iota(jnp.int32, (48, 1), 0)
    owner = lane // 4 == row48 // 2
    second = lax.rem(row48, 2) == 1
    moved = jnp.zeros((144, 128), F32)
    for q in range(0, 18, 2):
        wide, fold = [], []
        for h in (q, q + 1):
            v = jnp.where(second, q_ref[2 * h + 1 : 2 * h + 2, :], q_ref[2 * h : 2 * h + 1, :])
            wide.append(jnp.concatenate(split3(jnp.where(owner, v, 0.0)), axis=0).astype(BF16))
            fold.append(jnp.where(lane == 4 * h + lax.rem(row, 4), 1.0, 0.0).astype(BF16))
        moved += dot(jnp.concatenate(wide, axis=1), jnp.concatenate(fold, axis=0))
    moved = moved[0:48] + moved[48:96] + moved[96:144]
    for p in range(NC):
        msg0[p] = moved[2 * p : 2 * p + 2]
    for c in range(4):
        pair = src_in[c].astype(F32)
        sends[c : c + 1, :] = jnp.concatenate([pair[0:1], pair[1:2]], axis=1)
    pl.semaphore_wait(barrier, NC + NX * NY - 2)
    ex0 = ring(NC, col, to_c, lambda p: msg0.at[p], buf0, s0, r0)
    push(ex0)
    buf0[col] = msg0[col]

    exs = plane(sends, bufs, ss, rs)
    push(exs)
    bufs[sub] = sends[...]

    fetches[0].wait()
    fetches[1].wait()
    e0, e1 = ends_ref[0:1, :], ends_ref[1:2, :]
    flip = e0 >= NS
    ends_row = jnp.concatenate([jnp.where(flip, e1, e0), jnp.where(flip, e0, e1)], axis=1)
    st_row = jnp.concatenate([node_ref[...], jnp.zeros((1, 80), jnp.int32)], axis=1)
    st_row = jnp.where(station_lane, st_row, -1 - lane)
    ends_col = jnp.broadcast_to(ends_row, (128, 128)).T
    st_col = jnp.broadcast_to(st_row, (128, 128)).T
    col192 = jnp.concatenate([ends_col, st_col[0:64]], axis=0)

    place = lax.rem(col192, NS)
    fetches[2].wait()
    acc = jnp.zeros((192, 128), F32)
    for k in range(0, NS, 256):
        halves = [jnp.where(place == lane + (k + h), 1.0, 0.0).astype(BF16) for h in (0, 128)]
        acc += lax.dot_general(
            jnp.concatenate(halves, axis=1), inv_ref[:, k : k + 256], NT, preferred_element_type=F32
        )
    gt = jnp.where((col192 >= NS) == jnp.broadcast_to(lane >= 64, (192, 128)), acc, 0.0)
    gt_ref[...] = gt

    gid = jnp.where(row >= 64, NS - 64, 0) + row + sub * 64
    st_high = pltpu.roll(st_row, 64, 1)
    row0 = jnp.where(low, ends_row, st_high)
    row1 = jnp.where(low, pltpu.roll(ends_row, 64, 1), st_high)
    pick = jnp.where(gid == jnp.where(row >= 64, row1, row0), 1.0, 0.0).astype(BF16)
    piece = lax.rem(z, 6) * 2 + core
    mine = gt_ref[pl.ds(pl.multiple_of(piece * 16, 16), 16), :]
    send1y[...] = dot(mine.astype(BF16), pick).astype(BF16)

    ex1y = ring(NY, y, to_y, lambda p: send1y, buf1y, s1y, r1y)
    push(ex1y)
    buf1y[y] = send1y[...]

    nrow = jnp.concatenate([ends_row, st_row], axis=1)
    ncol = jnp.concatenate([twice_over(ends_col), twice_over(st_col)], axis=0)
    b_row = lax.broadcasted_iota(jnp.int32, (256, 256), 0)
    b_col = lax.broadcasted_iota(jnp.int32, (256, 256), 1)
    equal = ncol == nrow
    earlier = jnp.where(equal & (b_row < b_col), 1.0, 0.0)
    leads = jnp.sum(earlier, axis=0, keepdims=True) == 0.0
    merge = jnp.where(equal & leads, 1.0, 0.0).astype(BF16)
    at_ends = jnp.where(gid == ends_row, 1.0, 0.0).astype(BF16)
    at_st = jnp.where(gid == st_row, 1.0, 0.0).astype(BF16)
    for i in range(6, 11):
        fetches[i].wait()
    delay = twice_over(delay_ref[...])
    twice = 2.0 * twice_over(admit_ref[...])
    in_service = twice_over(breaker_ref[...].astype(F32))
    flips = twice_over(jnp.where(flip, 1, 0))
    end_of = 2 * jnp.where(low, lane, lane - 64) + jnp.where(low, flips, 1 - flips)
    perm = jnp.where(row == end_of, 1.0, 0.0).astype(BF16)
    hist = jnp.concatenate([hv_ref[t] for t in range(DMAX)] + [hj_ref[t] for t in range(DMAX)], axis=0)
    hist = dot(jnp.concatenate(split3(hist), axis=0).astype(BF16), perm)
    hist = hist[0:48] + hist[48:96] + hist[96:144]
    volts = [hist[4 * t : 4 * t + 4] for t in range(DMAX)]
    injs = [hist[24 + 4 * t : 28 + 4 * t] for t in range(DMAX)]

    await_recv(exs)
    for p in range(NY):
        for q in range(NX // 2):
            a = bufs[4 * p + 2 * q]
            b = bufs[4 * p + 2 * q + 1]
            m = (2 * p + q) * 128
            s_ref[0:4, m : m + 128] = jnp.where(low, a, pltpu.roll(b, 64, 1))
            s_ref[4:8, m : m + 128] = jnp.where(low, pltpu.roll(a, 64, 1), b)
    both = lax.dot_general(s_ref[...].astype(BF16), inv_ref[...], NT, preferred_element_type=F32)
    source_part = jnp.where(low, both[0:4], both[4:8])
    send2y[16:20, :] = exact_dot(source_part, at_ends)
    send2y[20:24, :] = exact_dot(source_part, at_st)

    await_recv(ex0)
    t_ref[...] = jnp.zeros((128, 128), F32)
    for p in range(NC):
        t_ref[2 * p : 2 * p + 2, :] = buf0[p]
    stations = t_ref[...].T
    send2y[0:16, :] = jnp.where(low, stations[0:16], pltpu.roll(stations[16:32], 64, 1))
    ex2y = ring(NY, y, to_y, lambda p: send2y, buf2y, s2y, r2y)
    push(ex2y)
    buf2y[y] = send2y[...]

    await_recv(ex1y)
    parts = [buf1y[p].astype(F32) for p in range(NY)]
    total = parts[0]
    for part in parts[1:]:
        total += part
    send1x[...] = total.astype(BF16)
    ex1x = ring(NX, x, to_x, lambda p: send1x, buf1x, s1x, r1x)
    push(ex1x)
    buf1x[x] = send1x[...]

    await_recv(ex1x)
    parts = [buf1x[p].astype(F32) for p in range(NX)]
    block = parts[0]
    for part in parts[1:]:
        block += part
    wsend[...] = block.astype(BF16)
    exw = []
    for dz in (1, -1, 2, -2, 3, 0):
        for dk in (0, 1):
            if dz or dk:
                k_to = lax.rem(core + dk, 2)
                z_to, z_from = lax.rem(z + dz + 12, 12), lax.rem(z - dz + 12, 12)
                exw.append(
                    ({"col": z_to * 2 + k_to}, lax.rem(z_from, 6) * 2 + k_to, piece, wsend, wbuf, sw, rw)
                )
    push(exw)
    wbuf[piece] = wsend[...]

    await_recv(ex2y)
    total = buf2y[0]
    for p in range(1, NY):
        total += buf2y[p]
    send2x[...] = total
    ex2x = ring(NX, x, to_x, lambda p: send2x, buf2x, s2x, r2x)
    push(ex2x)
    buf2x[x] = total

    await_recv(exw)
    w = jnp.concatenate([wbuf[p].astype(F32) for p in range(12)], axis=0)
    high_w = pltpu.roll(w, 64, 1)
    is_high = col192 >= NS
    w_ends = jnp.where(low, jnp.where(is_high, 0.0, w), jnp.where(is_high, high_w, 0.0))
    w_st = jnp.where(low, high_w, 0.0)
    w_full = jnp.concatenate(
        [jnp.concatenate([w_ends, w_st], axis=1), jnp.zeros((64, 256), F32)], axis=0
    ).astype(BF16)

    await_recv(ex2x)
    total = buf2x[0]
    for p in range(1, NX):
        total += buf2x[p]
    sums = jnp.where(
        station_lane,
        jnp.concatenate([total[0:16], pltpu.roll(total[0:16], 64, 1)], axis=0),
        0.0,
    )
    src_nodes = jnp.concatenate([total[16:20], total[20:24]], axis=1)

    counts = [jnp.where(station_lane, stations[32 + 4 * n : 36 + 4 * n], 0.0) for n in range(STEPS)]
    node_volt = jnp.where(station_lane, stations[64:68], 0.0)
    currents = []
    for n in range(STEPS):
        u, j = volts[n + DMAX - DMIN], injs[n + DMAX - DMIN]
        for d in range(DMIN + 1, DMAX + 1):
            u = jnp.where(delay == d, volts[n + DMAX - d], u)
            j = jnp.where(delay == d, injs[n + DMAX - d], j)
        injection = in_service * (twice * pltpu.roll(u, 64, 1) - pltpu.roll(j, 64, 1))
        injs.append(injection)
        charge = sums[4 * n : 4 * n + 4]
        for q in range(n):
            charge -= 0.5 * jnp.minimum(counts[n], counts[q]) * currents[q]
        current = (2.0 / SM * charge - node_volt) / (1.0 + counts[n] / SM)
        current = jnp.where(station_lane, current, 0.0)
        currents.append(current)
        term = exact_dot(jnp.concatenate([injection, current], axis=1), merge)
        term = jnp.concatenate([term, jnp.zeros_like(term)], axis=0).astype(BF16)
        if n + 1 < STEPS:
            nodes = dot(term, w_full)[0:4] + src_nodes
            volts.append(nodes[:, 0:128])
            node_volt = nodes[:, 128:256]

    t_ref[0:32, :] = jnp.concatenate(currents, axis=0)
    t_ref[32:128, :] = jnp.zeros((96, 128), F32)
    out = t_ref[...].T
    for p in range(NC):
        send3[p] = out[2 * p : 2 * p + 2, :]
    ex3 = ring(NC, col, to_c, lambda p: send3.at[p], buf3, s3, r3)
    push(ex3)
    buf3[col] = send3[col]
    last = dot(term, jnp.concatenate([gt, jnp.zeros((64, 128), F32)], axis=0).astype(BF16))
    final = source_part + last[0:4]
    for c in range(4):
        volt_ref[c] = jnp.concatenate([final[c : c + 1, 0:64], final[c : c + 1, 64:128]], axis=0)
    spread = [jnp.where(row == 4 * n + lax.rem(lane, 4), 1.0, 0.0).astype(BF16) for n in range(STEPS)]
    spread = jnp.concatenate(spread, axis=1)
    for ex in (ex0, exs, ex1y, ex1x, exw, ex2y, ex2x):
        await_send(ex)
    await_recv(ex3)
    for p in range(NC):
        t_ref[2 * p : 2 * p + 2, :] = buf3[p]
    wide = dot(jnp.concatenate(split3(t_ref[0:48, :]), axis=0).astype(BF16), spread)
    wide = wide[0:48] + wide[48:96] + wide[96:144]
    discharge = jnp.zeros((75, 2, 96), F32)
    for n in range(STEPS):
        tile = jnp.where(owner, wide[:, 128 * n : 128 * n + 128], 0.0)
        rows = [jnp.sum(jnp.where(second == s, tile, 0.0), axis=0, keepdims=True) for s in (False, True)]
        current = jnp.concatenate(rows, axis=0)[:, 0:96]
        cur_out[n] = current
        discharge += jnp.where(position < count_ref[n][None], current[None], 0.0)
    cap_out[...] = cap_ref[...] - 0.5 * discharge
    await_send(ex3)


def write_kernel(a, b, c, x, y, z, sems):
    pieces = [(a, x), (c, z)] + [(b.at[pl.ds(k, 15)], y.at[pl.ds(k, 15)]) for k in range(0, 75, 15)]
    copies = [pltpu.make_async_copy(s, d, sems.at[i]) for i, (s, d) in enumerate(pieces)]
    for copy in copies:
        copy.start()
    for copy in copies:
        copy.wait()


def exchange(*inputs):
    vmem, hbm = pl.BlockSpec(memory_space=pltpu.VMEM), pl.BlockSpec(memory_space=HBM)
    pairs = lambda n: [pltpu.SemaphoreType.DMA((n,)), pltpu.SemaphoreType.DMA((n,))]
    outs = tuple(jax.ShapeDtypeStruct(s, F32) for s in ((4, 2, 64), (75, 2, 96), (STEPS, 2, 96)))
    fetched = [inputs[0]] + list(inputs[2:])
    results = pl.pallas_call(
        kernel,
        out_shape=outs,
        in_specs=[hbm, vmem] + [hbm] * 10,
        out_specs=(vmem,) * 3,
        scratch_shapes=[
            *(pltpu.VMEM(v.shape, v.dtype) for v in fetched),
            pltpu.VMEM((192, 128), F32),
            pltpu.VMEM((8, NS), F32),
            pltpu.VMEM((128, 128), F32),
            pltpu.VMEM((40, 128), F32),
            pltpu.VMEM((4, 128), F32),
            pltpu.VMEM((NX * NY, 4, 128), F32),
            pltpu.VMEM((16, 128), BF16),
            pltpu.VMEM((NY, 16, 128), BF16),
            pltpu.VMEM((16, 128), BF16),
            pltpu.VMEM((NX, 16, 128), BF16),
            pltpu.VMEM((16, 128), BF16),
            pltpu.VMEM((12, 16, 128), BF16),
            pltpu.VMEM((NC, 2, 128), F32),
            pltpu.VMEM((NC, 2, 128), F32),
            pltpu.VMEM((24, 128), F32),
            pltpu.VMEM((NY, 24, 128), F32),
            pltpu.VMEM((24, 128), F32),
            pltpu.VMEM((NX, 24, 128), F32),
            pltpu.VMEM((NC, 2, 128), F32),
            pltpu.VMEM((NC, 2, 128), F32),
            pltpu.SemaphoreType.DMA((11,)),
            *pairs(NC), *pairs(NX * NY), *pairs(NY), *pairs(NX), *pairs(12), *pairs(NY), *pairs(NX), *pairs(NC),
        ],
        compiler_params=pltpu.CompilerParams(
            collective_id=0, has_side_effects=True, vmem_limit_bytes=60 * 1024 * 1024
        ),
    )(*inputs)
    return pl.pallas_call(
        write_kernel,
        out_shape=outs,
        in_specs=[vmem] * 3,
        out_specs=(hbm,) * 3,
        scratch_shapes=[pltpu.SemaphoreType.DMA((7,))],
        compiler_params=pltpu.CompilerParams(vmem_limit_bytes=60 * 1024 * 1024),
    )(*results)


def per_device(
    inv_conductance, source, line_ends, delays, admittance, breaker, hist_volt, hist_inj,
    station_node, station_initial, capacitor_initial, insert_count,
):
    volts, capacitor, current = exchange(
        inv_conductance.reshape(128, NS), source, line_ends.T, delays[None, :], admittance[None, :],
        breaker.T, hist_volt, hist_inj, station_node[None, :], station_initial.T,
        capacitor_initial.transpose(2, 1, 0), insert_count.transpose(0, 2, 1),
    )
    return volts, capacitor.transpose(2, 1, 0), current.transpose(0, 2, 1)


def solution(mesh):
    in_specs = (
        P(None, "sub", None),
        P("col", None, "sub"),
        P(),
        P(),
        P(),
        P(None, "col"),
        P(None, "col", None),
        P(None, "col", None),
        P(),
        P(None, "col"),
        P(None, "col", "sub"),
        P(None, None, "col"),
    )
    out_specs = (P("col", None, "sub"), P(None, "col", "sub"), P(None, None, "col"))
    return jax.shard_map(
        per_device, mesh=mesh, in_specs=in_specs, out_specs=out_specs, check_vma=False
    )
```
